32 devices in a mesh: groups: 2 (over y), batch: 4 (over z), mp: 4 (over x, core).
Axes of the slice: x: 2, y: 2, z: 4, core: 2. Of those that a mesh axis runs over, the one named last changes fastest.
Arguments:
- tokens: bfloat16 [192, 18432], P(('groups', 'batch'), 'mp'), parts along dimension 0, may hold values from -3000 to 3000
- norm_gain: float32 [18432], P('mp'), may hold values from 0.1 to 1.9
- w_qkv: bfloat16 [18432, 12800], P('mp', 'batch'), may hold values from -0.046875 to 0.046875
- key_cache: bfloat16 [192, 512, 256], P(('groups', 'batch', 'mp')), parts along dimension 0, may hold values from -200 to 200
- value_cache: bfloat16 [192, 512, 256], P(('groups', 'batch', 'mp')), parts along dimension 0, may hold values from -6 to 6
- lengths: int32 [192], P(('groups', 'batch', 'mp')), parts along dimension 0, may hold values from 1 to 512, as said below
Outputs:
- context: bfloat16 [192, 12288], P(('groups', 'batch', 'mp')), parts along dimension 0
The draws below stay inside these ranges and needn't reach their ends.
There are 2 independent parts, one for each index of `groups`. The reference program is written for one: setup_inputs(seed, part) draws one part's arguments, and reference() takes and returns one part's arrays. A program takes and returns all parts, laid end to end along the dimension named above; an argument that names none is the same for every part. Nothing has to cross between parts.
Inputs may be any that keep to these rules, and one draw needn't show every extreme that they name: `lengths`: some row uses all 512 positions and some row uses one.
All inputs are finite; a program needn't handle non-finite values.
Results may differ from the reference program's by a relative error of at most 0.0033.
The reference program's roundings to bfloat16 on the way (of `normed`, `raw_qkv`, `queries` and `weights_low`) count: a program that leaves them out, or rounds other values in their place, can miss the bound.
Values may be sent and summed in bfloat16 or wider, within the bound.
A program may use at most 128 MiB of HBM per device.

```python
import math
import jax
import jax.numpy as jnp
from jax import lax

D = 18432
HQ = 48
HD = 256
CTX = 512
ROWS = 96
QKV = 12800


def draw_tokens(key, part):
    key = jax.random.fold_in(key, 11)
    key_base, key_rows, key_cols = jax.random.split(key, 3)
    ramp = 3.0 ** (jnp.arange(D, dtype=jnp.float32) / D)
    col_scale = jnp.exp(jax.random.uniform(key_cols, (1, D), jnp.float32, 0.0, math.log(10.0))) * ramp[None, :]
    entries = jnp.clip(jax.random.normal(key_base, (ROWS, D), jnp.float32), -6.0, 6.0)
    row_scale = jnp.exp(jax.random.uniform(key_rows, (ROWS, 1), jnp.float32, 0.0, math.log(10.0)))
    return (entries * row_scale * col_scale).astype(jnp.bfloat16)


def draw_key_cache(key, part):
    key = jax.random.fold_in(key, 23)
    key_base = jax.random.fold_in(key, 0)
    entries = jnp.clip(jax.random.normal(key_base, (ROWS, CTX, HD), jnp.float32), -6.0, 6.0)
    return entries.astype(jnp.bfloat16)


def draw_lengths(key, part):
    key = jax.random.fold_in(key, 37)
    key_counts, key_long, key_offset = jax.random.split(key, 3)
    counts = jax.random.randint(key_counts, (ROWS,), 1, CTX + 1, dtype=jnp.int32)
    longest = jax.random.randint(key_long, (), 0, ROWS, dtype=jnp.int32)
    offset = jax.random.randint(key_offset, (), 1, ROWS, dtype=jnp.int32)
    shortest = (longest + offset) % ROWS
    counts = counts.at[longest].set(CTX)
    counts = counts.at[shortest].set(1)
    return counts


def level_of(own_key, shape, shards, smallest, high):
    loudness, own = 1.0, jax.random.fold_in(own_key, 6)
    for dim, shards_of in shards:
        draws = jnp.exp(jax.random.uniform(jax.random.fold_in(own, dim), (shards_of,), jnp.float32, smallest / len(shards), high / len(shards)))
        loudness = loudness * jnp.repeat(draws, shape[dim] // shards_of).reshape([-1 if axis == dim else 1 for axis in range(len(shape))])
    return loudness


def scatter_about(stream_key, extent, scale, limit, pieces=(), kind=jnp.bfloat16):
    gain = level_of(stream_key, extent, pieces, -0.22, 0.18) if pieces else 1.0
    result = jax.random.normal(stream_key, extent, jnp.float32) * scale * gain
    return jnp.minimum(jnp.maximum(result, -limit), limit).astype(kind)


def setup_inputs(seed: int = 0, part: int = 0) -> dict:
    key_list = jax.random.split(jax.random.key(seed), 7)
    part_splits = jax.random.split(jax.random.fold_in(key_list[6], part), 7)
    tokens = draw_tokens(jax.random.fold_in(jax.random.fold_in(key_list[6], part), 71), part)
    norm_gain = jnp.clip(1.0 + 0.18 * jax.random.normal(key_list[1], (D,), jnp.float32), 0.1, 1.9)
    w_qkv = scatter_about(key_list[2], (D, QKV), D ** -0.5, 0.046875, ((0, 4), (1, 4)))
    key_cache = draw_key_cache(jax.random.fold_in(jax.random.fold_in(key_list[6], part), 71), part)
    value_cache = scatter_about(part_splits[4], (ROWS, CTX, HD), 1.0, 6.0, ((0, 16),))
    lengths = draw_lengths(jax.random.fold_in(jax.random.fold_in(key_list[6], part), 71), part)
    return {"tokens": tokens, "norm_gain": norm_gain, "w_qkv": w_qkv, "key_cache": key_cache, "value_cache": value_cache, "lengths": lengths}


EPSILON = 1e-06
NEG_FILL = -1e+30

def attend_block(items):
    queries, key_block, value_block, new_key, new_value, inv_rms, row_lengths = items
    query_float = queries.astype(jnp.float32)
    scale = inv_rms[:, None, None] / math.sqrt(HD)
    scores = jnp.einsum('rhd,rpd->rhp', query_float, key_block.astype(jnp.float32)) * scale
    own_score = jnp.einsum('rhd,rd->rh', query_float, new_key.astype(jnp.float32)) * (inv_rms * inv_rms / math.sqrt(HD))[:, None]
    positions = jnp.arange(key_block.shape[1], dtype=jnp.int32)
    valid_mask = (positions[None, :] < row_lengths[:, None])[:, None, :]
    scores = jnp.where(valid_mask, scores, NEG_FILL)
    row_max = jnp.maximum(lax.optimization_barrier(jnp.max(scores, axis=2)), own_score)
    weights = jnp.where(valid_mask, jnp.exp(scores - row_max[:, :, None]), 0.0)
    own_weight = jnp.exp(own_score - row_max)
    denominator = lax.optimization_barrier(jnp.sum(weights, axis=2)) + own_weight
    weights_low = lax.optimization_barrier(weights.astype(jnp.bfloat16))
    weighted = jnp.einsum('rhp,rpd->rhd', weights_low.astype(jnp.float32), value_block.astype(jnp.float32))
    weighted = weighted + own_weight[:, :, None] * inv_rms[:, None, None] * new_value.astype(jnp.float32)[:, None, :]
    context = weighted / denominator[:, :, None]
    return context.astype(jnp.bfloat16).reshape(queries.shape[0], HQ * HD)

def reference(tokens, norm_gain, w_qkv, key_cache, value_cache, lengths):
    widened = tokens.astype(jnp.float32)
    normed = (widened * norm_gain).astype(jnp.bfloat16)
    inv_rms = 1.0 / jnp.sqrt(lax.optimization_barrier(jnp.sum(widened * widened, axis=1)) / D + EPSILON)
    raw_qkv = jnp.dot(normed, w_qkv, preferred_element_type=jnp.float32).astype(jnp.bfloat16)
    queries = raw_qkv[:, :HQ * HD].reshape(ROWS, HQ, HD)
    new_key = raw_qkv[:, HQ * HD:HQ * HD + HD]
    new_value = raw_qkv[:, HQ * HD + HD:]
    block_rows = math.gcd(ROWS, 64)
    count = ROWS // block_rows

    def split_rows(array):
        return array.reshape((count, block_rows) + array.shape[1:])
    items = (split_rows(queries), split_rows(key_cache), split_rows(value_cache), split_rows(new_key), split_rows(new_value), split_rows(inv_rms), split_rows(lengths))
    return lax.map(attend_block, items).reshape(ROWS, HQ * HD)
```

```python
import math

import jax
import jax.numpy as jnp
from jax import lax
from jax.experimental import pallas as pl
from jax.experimental.pallas import tpu as pltpu
from jax.sharding import PartitionSpec as P

D = 18432
HQ = 48
HD = 256


EPSILON = 1e-06
NEG_FILL = -1e30

BATCH = 4
MODEL = 4
ROWS = 24
SHARE = 6
HALF = 256
CHUNK = 2 * HALF
LANES = 128
PIECE = 5
PIECE_COLS = PIECE * LANES
PIECE_ROWS = 32
HEAD_ROWS = 64
MESH_ID = pl.DeviceIdType.MESH


def attend(raw_qkv, inv_rms, key_cache, value_cache, lengths):
    row_count = raw_qkv.shape[0]
    queries = raw_qkv[:, : HQ * HD].reshape(row_count, HQ, HD)
    new_key = raw_qkv[:, HQ * HD : HQ * HD + HD]
    new_value = raw_qkv[:, HQ * HD + HD :]
    scale = inv_rms[:, None, None] / math.sqrt(HD)
    scores = (
        jnp.einsum("rhd,rpd->rhp", queries, key_cache, preferred_element_type=jnp.float32) * scale
    )
    own_score = (
        jnp.einsum("rhd,rd->rh", queries, new_key, preferred_element_type=jnp.float32)
        * (inv_rms * inv_rms / math.sqrt(HD))[:, None]
    )
    positions = jnp.arange(key_cache.shape[1], dtype=jnp.int32)
    valid_mask = (positions[None, :] < lengths[:, None])[:, None, :]
    scores = jnp.where(valid_mask, scores, NEG_FILL)
    row_max = jnp.maximum(jnp.max(scores, axis=2), own_score)
    weights = jnp.where(valid_mask, jnp.exp(scores - row_max[:, :, None]), 0.0)
    own_weight = jnp.exp(own_score - row_max)
    denominator = jnp.sum(weights, axis=2) + own_weight
    weights_low = weights.astype(jnp.bfloat16)
    weighted = jnp.einsum(
        "rhp,rpd->rhd", weights_low, value_cache, preferred_element_type=jnp.float32
    )
    weighted = (
        weighted
        + own_weight[:, :, None]
        * inv_rms[:, None, None]
        * new_value.astype(jnp.float32)[:, None, :]
    )
    context = weighted / denominator[:, :, None]
    return context.astype(jnp.bfloat16).reshape(row_count, HQ * HD)


def plain_device(tokens, norm_gain, w_qkv, key_cache, value_cache, lengths):
    widened = tokens.astype(jnp.float32)
    normed = (widened * norm_gain).astype(jnp.bfloat16)
    square_part = jnp.sum(widened * widened, axis=1)
    partial_value = jnp.dot(
        lax.all_gather(normed, "batch", axis=0, tiled=True),
        w_qkv,
        preferred_element_type=jnp.float32,
    )
    batch_count = lax.axis_size("batch")
    model_count = lax.axis_size("mp")
    row_total = tokens.shape[0]
    row_share = row_total // model_count
    col_width = w_qkv.shape[1]
    blocks = partial_value.reshape(batch_count, model_count, row_share, col_width)
    summed, square_sum = (
        lax.psum_scatter(blocks, "mp", scatter_dimension=1, tiled=True),
        lax.psum_scatter(
            square_part.reshape(1, model_count, row_share), "mp", scatter_dimension=1, tiled=True
        ),
    )
    arrived = lax.all_to_all(
        summed.astype(jnp.bfloat16), "batch", split_axis=0, concat_axis=3, tiled=True
    )
    raw_qkv = arrived.reshape(row_share, batch_count * col_width)
    square_sum = square_sum.reshape(row_share)
    inv_rms = 1.0 / jnp.sqrt(square_sum / D + EPSILON)
    return attend(raw_qkv, inv_rms, key_cache, value_cache, lengths)


def one_hot(source, width):
    lanes = lax.broadcasted_iota(jnp.int32, (source.shape[0], width), 1)
    return jnp.where(lanes == source, 1.0, 0.0).astype(jnp.bfloat16)


def row_index(count):
    return lax.broadcasted_iota(jnp.int32, (count, 1), 0)


def gather_matrix():
    index = row_index(2 * BATCH * ROWS)
    half = lax.div(index, BATCH * ROWS)
    place = lax.rem(index, BATCH * ROWS)
    core = lax.div(place, 2 * ROWS)
    along_x = lax.rem(lax.div(place, ROWS), 2)
    batch = lax.div(lax.rem(place, ROWS), SHARE)
    row = lax.rem(place, SHARE)
    source = batch * (2 * ROWS) + half * ROWS + (along_x * 2 + core) * SHARE + row
    return one_hot(source, 2 * BATCH * ROWS)


def scatter_matrix():
    index = row_index(BATCH * PIECE_ROWS)
    batch = lax.div(index, PIECE_ROWS)
    within = lax.rem(index, PIECE_ROWS)
    block = lax.div(within, SHARE)
    row = lax.rem(within, SHARE)
    source = jnp.where(within < PIECE * SHARE, block * ROWS + batch * SHARE + row, -1)
    return one_hot(source, LANES)


def head_matrix(row, width):
    index = row_index(2 * HEAD_ROWS)
    half = lax.div(index, HEAD_ROWS)
    head = lax.rem(index, HEAD_ROWS)
    block = head * 2 + half
    piece = lax.div(block, PIECE)
    source = piece * PIECE_ROWS + (block - piece * PIECE) * SHARE + row
    return one_hot(source, width)


def fused_kernel(
    lengths_ref, tokens_ref, gain_ref, w_ref, key_ref, value_ref, out_ref,
    w_buf, key_buf, value_buf, gathered, order, spread, heads, acc,
    core_in, x_out, x_in, z_out, z_in, squares, inverse,
    w_sem, cache_sem,
    right_send, right_recv, left_send, left_recv,
    core_send, core_recv, x_send, x_recv, z_send, z_recv, sq_send, sq_recv,
):
    group = lax.axis_index("groups")
    batch = lax.axis_index("batch")
    model = lax.axis_index("mp")
    core = lax.rem(model, 2)
    along_x = lax.div(model, 2)
    sibling = model + 1 - 2 * core
    across = lax.rem(model + 2, MODEL)
    chunks = w_ref.shape[0] // CHUNK
    pieces = w_ref.shape[1] // PIECE_COLS

    barrier = pltpu.get_barrier_semaphore()
    for step in range(1, BATCH):
        pl.semaphore_signal(
            barrier, inc=1, device_id=(group, lax.rem(batch + step, BATCH), model),
            device_id_type=MESH_ID,
        )
    for step in range(1, MODEL):
        pl.semaphore_signal(
            barrier, inc=1, device_id=(group, batch, lax.rem(model + step, MODEL)),
            device_id_type=MESH_ID,
        )

    def w_copy(k):
        return pltpu.make_async_copy(
            w_ref.at[pl.ds(pl.multiple_of(k * CHUNK, CHUNK), CHUNK)], w_buf.at[k], w_sem.at[k]
        )

    @pl.loop(0, chunks)
    def _(k):
        w_copy(k).start()

    key_copy = pltpu.make_async_copy(key_ref, key_buf, cache_sem.at[0])
    value_copy = pltpu.make_async_copy(value_ref, value_buf, cache_sem.at[1])
    key_copy.start()
    value_copy.start()

    total = jnp.zeros((ROWS, LANES), jnp.float32)
    for k in range(chunks):
        parts = []
        for half in range(2):
            columns = pl.ds(k * CHUNK + half * HALF, HALF)
            widened = tokens_ref[:, columns].astype(jnp.float32)
            parts.append(widened * gain_ref[:, columns])
            squared = widened * widened
            total = total + squared[:, :LANES] + squared[:, LANES:]
        gathered[k, batch] = jnp.concatenate(parts, axis=0).astype(jnp.bfloat16)
    squares[model] = jnp.broadcast_to(jnp.sum(total, axis=1, keepdims=True), (ROWS, LANES))

    pl.semaphore_wait(barrier, BATCH + MODEL - 2)

    def to_right(d, k):
        block = gathered.at[k, lax.max(batch - d, 0)]
        return pltpu.make_async_remote_copy(
            src_ref=block, dst_ref=block,
            send_sem=right_send.at[d, k], recv_sem=right_recv.at[d, k],
            device_id=(group, lax.min(batch + 1, BATCH - 1), model), device_id_type=MESH_ID,
        )

    def to_left(d, k):
        block = gathered.at[k, lax.min(batch + d, BATCH - 1)]
        return pltpu.make_async_remote_copy(
            src_ref=block, dst_ref=block,
            send_sem=left_send.at[d, k], recv_sem=left_recv.at[d, k],
            device_id=(group, lax.max(batch - 1, 0), model), device_id_type=MESH_ID,
        )

    def sends_right(d):
        return jnp.logical_and(batch >= d, batch < BATCH - 1)

    def sends_left(d):
        return jnp.logical_and(batch + d < BATCH, batch > 0)

    def send(d, k):
        pl.when(sends_right(d))(lambda: to_right(d, k).start())
        pl.when(sends_left(d))(lambda: to_left(d, k).start())

    def receive(d, k):
        incoming = gathered.at[k, 0]

        @pl.when(batch >= d + 1)
        def _():
            pltpu.make_async_remote_copy(
                src_ref=incoming, dst_ref=gathered.at[k, lax.max(batch - d - 1, 0)],
                send_sem=right_send.at[d, k], recv_sem=right_recv.at[d, k],
                device_id=(group, lax.max(batch - 1, 0), model), device_id_type=MESH_ID,
            ).wait_recv()
            if d + 1 < BATCH - 1:
                pl.when(batch < BATCH - 1)(lambda: to_right(d + 1, k).start())

        @pl.when(batch + d + 1 < BATCH)
        def _():
            pltpu.make_async_remote_copy(
                src_ref=incoming, dst_ref=gathered.at[k, lax.min(batch + d + 1, BATCH - 1)],
                send_sem=left_send.at[d, k], recv_sem=left_recv.at[d, k],
                device_id=(group, lax.min(batch + 1, BATCH - 1), model), device_id_type=MESH_ID,
            ).wait_recv()
            if d + 1 < BATCH - 1:
                pl.when(batch > 0)(lambda: to_left(d + 1, k).start())

    send(0, 0)
    send(0, 1)

    def square_copy(step):
        return pltpu.make_async_remote_copy(
            src_ref=squares.at[model], dst_ref=squares.at[model],
            send_sem=sq_send.at[step], recv_sem=sq_recv.at[step],
            device_id=(group, batch, lax.rem(model + step, MODEL)), device_id_type=MESH_ID,
        )

    for step in range(1, MODEL):
        square_copy(step).start()

    order[...] = gather_matrix()
    spread[...] = scatter_matrix()
    for row in range(SHARE):
        heads[row] = head_matrix(row, heads.shape[2])

    def left_side(k):
        arrived = gathered[k].reshape(2 * BATCH * ROWS, HALF)
        ordered = jnp.dot(order[...], arrived, preferred_element_type=jnp.float32)
        ordered = ordered.astype(jnp.bfloat16)
        return jnp.concatenate([ordered[: BATCH * ROWS], ordered[BATCH * ROWS :]], axis=1)

    acc[...] = jnp.zeros_like(acc)

    width = w_ref.shape[1]
    tile = 3 * HD

    @pl.loop(0, chunks + 1)
    def _(it):
        pl.when(it + 2 < chunks)(lambda: send(0, it + 2))
        pl.when(it < chunks)(lambda: receive(0, it))
        pl.when(jnp.logical_and(it >= 1, it < chunks + 1))(lambda: receive(1, it - 1))

        @pl.when(it >= 2)
        def _():
            k = it - 2
            receive(2, k)
            w_copy(k).wait()
            left = left_side(k)
            start = 0
            while start < width:
                stop = width if width - start < 2 * tile - LANES else start + tile
                acc[:, start:stop] += jnp.dot(
                    left, w_buf[k, :, start:stop], preferred_element_type=jnp.float32
                )
                start = stop

    last = chunks - 1
    receive(2, last)
    w_copy(last).wait()
    left = left_side(last)

    def half_rows(which):
        return pl.ds(pl.multiple_of(which * (2 * ROWS), 8), 2 * ROWS)

    def core_copy(j):
        return pltpu.make_async_remote_copy(
            src_ref=acc.at[half_rows(1 - core), pl.ds(j * PIECE_COLS, PIECE_COLS)],
            dst_ref=core_in.at[j],
            send_sem=core_send.at[j], recv_sem=core_recv.at[j],
            device_id=(group, batch, sibling), device_id_type=MESH_ID,
        )

    def x_copy(j):
        return pltpu.make_async_remote_copy(
            src_ref=x_out.at[j], dst_ref=x_in.at[j],
            send_sem=x_send.at[j], recv_sem=x_recv.at[j],
            device_id=(group, batch, across), device_id_type=MESH_ID,
        )

    def z_copy(j, step):
        other = lax.rem(batch + step, BATCH)
        return pltpu.make_async_remote_copy(
            src_ref=z_out.at[j, other], dst_ref=z_in.at[batch, j],
            send_sem=z_send.at[step, j], recv_sem=z_recv.at[step, j],
            device_id=(group, other, model), device_id_type=MESH_ID,
        )

    def pair_sum(j, which):
        rows = pl.ds(pl.multiple_of(core * (2 * ROWS) + which * ROWS, 8), ROWS)
        own = acc[rows, pl.ds(j * PIECE_COLS, PIECE_COLS)]
        return own + core_in[j, pl.ds(pl.multiple_of(which * ROWS, 8), ROWS)]

    def pass_across(j):
        core_copy(j).wait_recv()
        x_out[j] = pair_sum(j, 1 - along_x)
        x_copy(j).start()

    for j in range(pieces):
        columns = slice(j * PIECE_COLS, (j + 1) * PIECE_COLS)
        acc[:, columns] += jnp.dot(
            left, w_buf[last, :, columns], preferred_element_type=jnp.float32
        )
        core_copy(j).start()
        if j:
            pass_across(j - 1)
    pass_across(pieces - 1)

    for j in range(pieces):
        x_copy(j).wait_recv()
        final = pair_sum(j, along_x) + x_in[j]
        blocks = [final[:, h * LANES : (h + 1) * LANES] for h in range(PIECE)]
        blocks.append(jnp.zeros((LANES - PIECE * ROWS, LANES), jnp.float32))
        stacked = jnp.concatenate(blocks, axis=0).astype(jnp.bfloat16)
        placed = jnp.dot(spread[...], stacked, preferred_element_type=jnp.float32)
        z_out[j] = placed.astype(jnp.bfloat16).reshape(BATCH, PIECE_ROWS, LANES)
        for step in range(1, BATCH):
            z_copy(j, step).start()
        z_in[batch, j] = z_out[j, batch]

    for step in range(1, MODEL):
        square_copy(step).wait_recv()
    square_sum = squares[0] + squares[1] + squares[2] + squares[3]
    inverse[...] = 1.0 / jnp.sqrt(square_sum / D + EPSILON)
    key_copy.wait()
    value_copy.wait()
    for j in range(pieces):
        for step in range(1, BATCH):
            z_copy(j, step).wait_recv()

    columns = z_in[...].reshape(BATCH * pieces * PIECE_ROWS, LANES)
    positions = lax.broadcasted_iota(jnp.int32, (HQ, key_ref.shape[1]), 1)
    for row in range(SHARE):
        picked = jnp.dot(heads[row], columns, preferred_element_type=jnp.float32)
        joined = jnp.concatenate([picked[:HEAD_ROWS], picked[HEAD_ROWS:]], axis=1)
        queries = joined[:HQ]
        new_key = joined[HQ : HQ + 1]
        new_value = joined[HQ + 1 : HQ + 2]
        inv_rms = inverse[pl.ds(model * SHARE + row, 1), :][:, :1]
        scores = lax.dot_general(
            queries.astype(jnp.bfloat16), key_buf[row], (((1,), (1,)), ((), ())),
            preferred_element_type=jnp.float32,
        ) * (inv_rms / math.sqrt(HD))
        own_score = jnp.sum(queries * new_key, axis=1, keepdims=True) * (
            inv_rms * inv_rms / math.sqrt(HD)
        )
        valid = positions < lengths_ref[row]
        scores = jnp.where(valid, scores, NEG_FILL)
        row_max = jnp.maximum(jnp.max(scores, axis=1, keepdims=True), own_score)
        weights = jnp.where(valid, jnp.exp(scores - row_max), 0.0)
        own_weight = jnp.exp(own_score - row_max)
        denominator = jnp.sum(weights, axis=1, keepdims=True) + own_weight
        weighted = jnp.dot(
            weights.astype(jnp.bfloat16), value_buf[row], preferred_element_type=jnp.float32
        )
        weighted = weighted + own_weight * inv_rms * new_value
        out_ref[row] = (weighted / denominator).astype(jnp.bfloat16)

    @pl.loop(0, chunks)
    def _(k):
        for d in range(BATCH - 1):
            pl.when(sends_right(d))(lambda d=d: to_right(d, k).wait_send())
            pl.when(sends_left(d))(lambda d=d: to_left(d, k).wait_send())

    for step in range(1, MODEL):
        square_copy(step).wait_send()
    for j in range(pieces):
        core_copy(j).wait_send()
        x_copy(j).wait_send()
        for step in range(1, BATCH):
            z_copy(j, step).wait_send()


def fused_device(tokens, norm_gain, w_qkv, key_cache, value_cache, lengths):
    features, width = w_qkv.shape
    chunks = features // CHUNK
    pieces = width // PIECE_COLS
    dma = pltpu.SemaphoreType.DMA
    vmem = pl.BlockSpec(memory_space=pltpu.VMEM)
    hbm = pl.BlockSpec(memory_space=pl.ANY)
    hops = BATCH - 1
    context = pl.pallas_call(
        fused_kernel,
        out_shape=jax.ShapeDtypeStruct((SHARE, HQ, HD), jnp.bfloat16),
        in_specs=[pl.BlockSpec(memory_space=pltpu.SMEM), vmem, vmem, hbm, hbm, hbm],
        out_specs=vmem,
        scratch_shapes=[
            pltpu.VMEM((chunks, CHUNK, width), jnp.bfloat16),
            pltpu.VMEM(key_cache.shape, jnp.bfloat16),
            pltpu.VMEM(value_cache.shape, jnp.bfloat16),
            pltpu.VMEM((chunks, BATCH, 2 * ROWS, HALF), jnp.bfloat16),
            pltpu.VMEM((2 * BATCH * ROWS, 2 * BATCH * ROWS), jnp.bfloat16),
            pltpu.VMEM((BATCH * PIECE_ROWS, LANES), jnp.bfloat16),
            pltpu.VMEM((SHARE, 2 * HEAD_ROWS, BATCH * pieces * PIECE_ROWS), jnp.bfloat16),
            pltpu.VMEM((BATCH * ROWS, width), jnp.float32),
            pltpu.VMEM((pieces, 2 * ROWS, PIECE_COLS), jnp.float32),
            pltpu.VMEM((pieces, ROWS, PIECE_COLS), jnp.float32),
            pltpu.VMEM((pieces, ROWS, PIECE_COLS), jnp.float32),
            pltpu.VMEM((pieces, BATCH, PIECE_ROWS, LANES), jnp.bfloat16),
            pltpu.VMEM((BATCH, pieces, PIECE_ROWS, LANES), jnp.bfloat16),
            pltpu.VMEM((MODEL, ROWS, LANES), jnp.float32),
            pltpu.VMEM((ROWS, LANES), jnp.float32),
            dma((chunks,)), dma((2,)),
            dma((hops, chunks)), dma((hops, chunks)), dma((hops, chunks)), dma((hops, chunks)),
            dma((pieces,)), dma((pieces,)), dma((pieces,)), dma((pieces,)),
            dma((BATCH, pieces)), dma((BATCH, pieces)),
            dma((MODEL,)), dma((MODEL,)),
        ],
        compiler_params=pltpu.CompilerParams(
            collective_id=0, has_side_effects=True, vmem_limit_bytes=54 * 1024 * 1024
        ),
        name="qkv_attention",
    )(lengths, tokens, norm_gain.reshape(1, features), w_qkv, key_cache, value_cache)
    return context.reshape(SHARE, HQ * HD)


def per_device(tokens, norm_gain, w_qkv, key_cache, value_cache, lengths):
    fits = (
        lax.axis_size("batch") == BATCH
        and lax.axis_size("mp") == MODEL
        and tokens.shape[0] == ROWS
        and w_qkv.shape[0] % CHUNK == 0
        and w_qkv.shape[1] % PIECE_COLS == 0
        and w_qkv.shape[1] * BATCH == (HQ + 2) * HD
    )
    run = fused_device if fits else plain_device
    return run(tokens, norm_gain, w_qkv, key_cache, value_cache, lengths)


def solution(mesh):
    return jax.shard_map(
        per_device,
        mesh=mesh,
        in_specs=(
            P(("groups", "batch"), "mp"),
            P("mp"),
            P("mp", "batch"),
            P(("groups", "batch", "mp"), None, None),
            P(("groups", "batch", "mp"), None, None),
            P(("groups", "batch", "mp")),
        ),
        out_specs=P(("groups", "batch", "mp"), None),
        check_vma=False,
    )
```

```python
import math

import jax
import jax.numpy as jnp
from jax import lax
from jax.experimental import pallas as pl
from jax.experimental.pallas import tpu as pltpu
from jax.sharding import PartitionSpec as P

D = 18432
HQ = 48
HD = 256


EPSILON = 1e-06
NEG_FILL = -1e30

BATCH = 4
MODEL = 4
ROWS = 24
SHARE = 6
HALF = 256
CHUNK = 2 * HALF
LANES = 128
PIECE = 5
PIECE_COLS = PIECE * LANES
PIECE_ROWS = 32
HEAD_ROWS = 64
AHEAD = 4
LAG = 3
MESH_ID = pl.DeviceIdType.MESH


def attend(raw_qkv, inv_rms, key_cache, value_cache, lengths):
    row_count = raw_qkv.shape[0]
    queries = raw_qkv[:, : HQ * HD].reshape(row_count, HQ, HD)
    new_key = raw_qkv[:, HQ * HD : HQ * HD + HD]
    new_value = raw_qkv[:, HQ * HD + HD :]
    scale = inv_rms[:, None, None] / math.sqrt(HD)
    scores = (
        jnp.einsum("rhd,rpd->rhp", queries, key_cache, preferred_element_type=jnp.float32) * scale
    )
    own_score = (
        jnp.einsum("rhd,rd->rh", queries, new_key, preferred_element_type=jnp.float32)
        * (inv_rms * inv_rms / math.sqrt(HD))[:, None]
    )
    positions = jnp.arange(key_cache.shape[1], dtype=jnp.int32)
    valid_mask = (positions[None, :] < lengths[:, None])[:, None, :]
    scores = jnp.where(valid_mask, scores, NEG_FILL)
    row_max = jnp.maximum(jnp.max(scores, axis=2), own_score)
    weights = jnp.where(valid_mask, jnp.exp(scores - row_max[:, :, None]), 0.0)
    own_weight = jnp.exp(own_score - row_max)
    denominator = jnp.sum(weights, axis=2) + own_weight
    weights_low = weights.astype(jnp.bfloat16)
    weighted = jnp.einsum(
        "rhp,rpd->rhd", weights_low, value_cache, preferred_element_type=jnp.float32
    )
    weighted = (
        weighted
        + own_weight[:, :, None]
        * inv_rms[:, None, None]
        * new_value.astype(jnp.float32)[:, None, :]
    )
    context = weighted / denominator[:, :, None]
    return context.astype(jnp.bfloat16).reshape(row_count, HQ * HD)


def plain_device(tokens, norm_gain, w_qkv, key_cache, value_cache, lengths):
    widened = tokens.astype(jnp.float32)
    normed = (widened * norm_gain).astype(jnp.bfloat16)
    square_part = jnp.sum(widened * widened, axis=1)
    partial_value = jnp.dot(
        lax.all_gather(normed, "batch", axis=0, tiled=True),
        w_qkv,
        preferred_element_type=jnp.float32,
    )
    batch_count = lax.axis_size("batch")
    model_count = lax.axis_size("mp")
    row_total = tokens.shape[0]
    row_share = row_total // model_count
    col_width = w_qkv.shape[1]
    blocks = partial_value.reshape(batch_count, model_count, row_share, col_width)
    summed, square_sum = (
        lax.psum_scatter(blocks, "mp", scatter_dimension=1, tiled=True),
        lax.psum_scatter(
            square_part.reshape(1, model_count, row_share), "mp", scatter_dimension=1, tiled=True
        ),
    )
    arrived = lax.all_to_all(
        summed.astype(jnp.bfloat16), "batch", split_axis=0, concat_axis=3, tiled=True
    )
    raw_qkv = arrived.reshape(row_share, batch_count * col_width)
    square_sum = square_sum.reshape(row_share)
    inv_rms = 1.0 / jnp.sqrt(square_sum / D + EPSILON)
    return attend(raw_qkv, inv_rms, key_cache, value_cache, lengths)


def one_hot(source, width):
    lanes = lax.broadcasted_iota(jnp.int32, (source.shape[0], width), 1)
    return jnp.where(lanes == source, 1.0, 0.0).astype(jnp.bfloat16)


def row_index(count):
    return lax.broadcasted_iota(jnp.int32, (count, 1), 0)


def gather_matrix():
    index = row_index(2 * BATCH * ROWS)
    half = lax.div(index, BATCH * ROWS)
    place = lax.rem(index, BATCH * ROWS)
    core = lax.div(place, 2 * ROWS)
    along_x = lax.rem(lax.div(place, ROWS), 2)
    batch = lax.div(lax.rem(place, ROWS), SHARE)
    row = lax.rem(place, SHARE)
    source = batch * (2 * ROWS) + half * ROWS + (along_x * 2 + core) * SHARE + row
    return one_hot(source, 2 * BATCH * ROWS)


def scatter_matrix():
    index = row_index(BATCH * PIECE_ROWS)
    batch = lax.div(index, PIECE_ROWS)
    within = lax.rem(index, PIECE_ROWS)
    block = lax.div(within, SHARE)
    row = lax.rem(within, SHARE)
    source = jnp.where(within < PIECE * SHARE, block * ROWS + batch * SHARE + row, -1)
    return one_hot(source, LANES)


def head_matrix(row, width):
    index = row_index(2 * HEAD_ROWS)
    half = lax.div(index, HEAD_ROWS)
    head = lax.rem(index, HEAD_ROWS)
    block = head * 2 + half
    piece = lax.div(block, PIECE)
    source = piece * PIECE_ROWS + (block - piece * PIECE) * SHARE + row
    return one_hot(source, width)


def fused_kernel(
    lengths_ref, tokens_ref, gain_ref, w_ref, key_ref, value_ref, out_ref,
    w_buf, key_buf, value_buf, gathered, order, spread, heads, acc,
    core_in, x_out, x_in, z_out, z_in, squares, inverse,
    w_sem, cache_sem,
    right_send, right_recv, left_send, left_recv,
    core_send, core_recv, x_send, x_recv, z_send, z_recv, sq_send, sq_recv,
):
    group = lax.axis_index("groups")
    batch = lax.axis_index("batch")
    model = lax.axis_index("mp")
    core = lax.rem(model, 2)
    along_x = lax.div(model, 2)
    sibling = model + 1 - 2 * core
    across = lax.rem(model + 2, MODEL)
    chunks = w_ref.shape[0] // CHUNK
    pieces = w_ref.shape[1] // PIECE_COLS

    barrier = pltpu.get_barrier_semaphore()
    for step in range(1, BATCH):
        pl.semaphore_signal(
            barrier, inc=1, device_id=(group, lax.rem(batch + step, BATCH), model),
            device_id_type=MESH_ID,
        )
    for step in range(1, MODEL):
        pl.semaphore_signal(
            barrier, inc=1, device_id=(group, batch, lax.rem(model + step, MODEL)),
            device_id_type=MESH_ID,
        )

    def w_copy(k):
        return pltpu.make_async_copy(
            w_ref.at[pl.ds(pl.multiple_of(k * CHUNK, CHUNK), CHUNK)], w_buf.at[k], w_sem.at[k]
        )

    @pl.loop(0, chunks)
    def _(k):
        w_copy(k).start()

    key_copy = pltpu.make_async_copy(key_ref, key_buf, cache_sem.at[0])
    value_copy = pltpu.make_async_copy(value_ref, value_buf, cache_sem.at[1])
    key_copy.start()
    value_copy.start()

    total = jnp.zeros((ROWS, LANES), jnp.float32)
    for k in range(chunks):
        parts = []
        for half in range(2):
            columns = pl.ds(k * CHUNK + half * HALF, HALF)
            widened = tokens_ref[:, columns].astype(jnp.float32)
            parts.append(widened * gain_ref[columns][None, :])
            squared = widened * widened
            total = total + squared[:, :LANES] + squared[:, LANES:]
        gathered[k, batch] = jnp.concatenate(parts, axis=0).astype(jnp.bfloat16)
    squares[model] = jnp.broadcast_to(jnp.sum(total, axis=1, keepdims=True), (ROWS, LANES))

    pl.semaphore_wait(barrier, BATCH + MODEL - 2)

    def to_right(d, k):
        block = gathered.at[k, lax.max(batch - d, 0)]
        return pltpu.make_async_remote_copy(
            src_ref=block, dst_ref=block,
            send_sem=right_send.at[d, k], recv_sem=right_recv.at[d, k],
            device_id=(group, lax.min(batch + 1, BATCH - 1), model), device_id_type=MESH_ID,
        )

    def to_left(d, k):
        block = gathered.at[k, lax.min(batch + d, BATCH - 1)]
        return pltpu.make_async_remote_copy(
            src_ref=block, dst_ref=block,
            send_sem=left_send.at[d, k], recv_sem=left_recv.at[d, k],
            device_id=(group, lax.max(batch - 1, 0), model), device_id_type=MESH_ID,
        )

    def sends_right(d):
        return jnp.logical_and(batch >= d, batch < BATCH - 1)

    def sends_left(d):
        return jnp.logical_and(batch + d < BATCH, batch > 0)

    def send(d, k):
        pl.when(sends_right(d))(lambda: to_right(d, k).start())
        pl.when(sends_left(d))(lambda: to_left(d, k).start())

    def receive(d, k):
        incoming = gathered.at[k, 0]

        @pl.when(batch >= d + 1)
        def _():
            pltpu.make_async_remote_copy(
                src_ref=incoming, dst_ref=gathered.at[k, lax.max(batch - d - 1, 0)],
                send_sem=right_send.at[d, k], recv_sem=right_recv.at[d, k],
                device_id=(group, lax.max(batch - 1, 0), model), device_id_type=MESH_ID,
            ).wait_recv()
            if d + 1 < BATCH - 1:
                pl.when(batch < BATCH - 1)(lambda: to_right(d + 1, k).start())

        @pl.when(batch + d + 1 < BATCH)
        def _():
            pltpu.make_async_remote_copy(
                src_ref=incoming, dst_ref=gathered.at[k, lax.min(batch + d + 1, BATCH - 1)],
                send_sem=left_send.at[d, k], recv_sem=left_recv.at[d, k],
                device_id=(group, lax.min(batch + 1, BATCH - 1), model), device_id_type=MESH_ID,
            ).wait_recv()
            if d + 1 < BATCH - 1:
                pl.when(batch > 0)(lambda: to_left(d + 1, k).start())

    for k in range(AHEAD):
        send(0, k)

    def square_copy(step):
        return pltpu.make_async_remote_copy(
            src_ref=squares.at[model], dst_ref=squares.at[model],
            send_sem=sq_send.at[step], recv_sem=sq_recv.at[step],
            device_id=(group, batch, lax.rem(model + step, MODEL)), device_id_type=MESH_ID,
        )

    for step in range(1, MODEL):
        square_copy(step).start()

    order[...] = gather_matrix()
    spread[...] = scatter_matrix()
    for row in range(SHARE):
        heads[row] = head_matrix(row, heads.shape[2])

    def left_side(k):
        arrived = gathered[k].reshape(2 * BATCH * ROWS, HALF)
        ordered = jnp.dot(order[...], arrived, preferred_element_type=jnp.float32)
        ordered = ordered.astype(jnp.bfloat16)
        return jnp.concatenate([ordered[: BATCH * ROWS], ordered[BATCH * ROWS :]], axis=1)

    acc[...] = jnp.zeros_like(acc)

    width = w_ref.shape[1]
    tile = 3 * HD

    @pl.loop(0, chunks - 1 + 2 * LAG)
    def _(it):
        pl.when(it + AHEAD < chunks)(lambda: send(0, it + AHEAD))
        pl.when(it < chunks)(lambda: receive(0, it))
        pl.when(jnp.logical_and(it >= LAG, it < chunks + LAG))(lambda: receive(1, it - LAG))

        @pl.when(it >= 2 * LAG)
        def _():
            k = it - 2 * LAG
            receive(2, k)
            w_copy(k).wait()
            left = left_side(k)
            start = 0
            while start < width:
                stop = width if width - start < 2 * tile - LANES else start + tile
                acc[:, start:stop] += jnp.dot(
                    left, w_buf[k, :, start:stop], preferred_element_type=jnp.float32
                )
                start = stop

    last = chunks - 1
    receive(2, last)
    w_copy(last).wait()
    left = left_side(last)

    def half_rows(which):
        return pl.ds(pl.multiple_of(which * (2 * ROWS), 8), 2 * ROWS)

    def core_copy(j):
        return pltpu.make_async_remote_copy(
            src_ref=acc.at[half_rows(1 - core), pl.ds(j * PIECE_COLS, PIECE_COLS)],
            dst_ref=core_in.at[j],
            send_sem=core_send.at[j], recv_sem=core_recv.at[j],
            device_id=(group, batch, sibling), device_id_type=MESH_ID,
        )

    def x_copy(j):
        return pltpu.make_async_remote_copy(
            src_ref=x_out.at[j], dst_ref=x_in.at[j],
            send_sem=x_send.at[j], recv_sem=x_recv.at[j],
            device_id=(group, batch, across), device_id_type=MESH_ID,
        )

    def z_copy(j, step):
        other = lax.rem(batch + step, BATCH)
        return pltpu.make_async_remote_copy(
            src_ref=z_out.at[j, other], dst_ref=z_in.at[batch, j],
            send_sem=z_send.at[step, j], recv_sem=z_recv.at[step, j],
            device_id=(group, other, model), device_id_type=MESH_ID,
        )

    def pair_sum(j, which):
        rows = pl.ds(pl.multiple_of(core * (2 * ROWS) + which * ROWS, 8), ROWS)
        own = acc[rows, pl.ds(j * PIECE_COLS, PIECE_COLS)]
        return own + core_in[j, pl.ds(pl.multiple_of(which * ROWS, 8), ROWS)]

    def pass_across(j):
        core_copy(j).wait_recv()
        x_out[j] = pair_sum(j, 1 - along_x)
        x_copy(j).start()

    for j in range(pieces):
        columns = slice(j * PIECE_COLS, (j + 1) * PIECE_COLS)
        acc[:, columns] += jnp.dot(
            left, w_buf[last, :, columns], preferred_element_type=jnp.float32
        )
        core_copy(j).start()
        if j:
            pass_across(j - 1)
    pass_across(pieces - 1)

    for j in range(pieces):
        x_copy(j).wait_recv()
        final = pair_sum(j, along_x) + x_in[j]
        blocks = [final[:, h * LANES : (h + 1) * LANES] for h in range(PIECE)]
        blocks.append(jnp.zeros((LANES - PIECE * ROWS, LANES), jnp.float32))
        stacked = jnp.concatenate(blocks, axis=0).astype(jnp.bfloat16)
        placed = jnp.dot(spread[...], stacked, preferred_element_type=jnp.float32)
        z_out[j] = placed.astype(jnp.bfloat16).reshape(BATCH, PIECE_ROWS, LANES)
        for step in range(1, BATCH):
            z_copy(j, step).start()
        z_in[batch, j] = z_out[j, batch]

    for step in range(1, MODEL):
        square_copy(step).wait_recv()
    square_sum = squares[0] + squares[1] + squares[2] + squares[3]
    inverse[...] = 1.0 / jnp.sqrt(square_sum / D + EPSILON)
    key_copy.wait()
    value_copy.wait()
    for j in range(pieces):
        for step in range(1, BATCH):
            z_copy(j, step).wait_recv()

    columns = z_in[...].reshape(BATCH * pieces * PIECE_ROWS, LANES)
    positions = lax.broadcasted_iota(jnp.int32, (HQ, key_ref.shape[1]), 1)
    for row in range(SHARE):
        picked = jnp.dot(heads[row], columns, preferred_element_type=jnp.float32)
        joined = jnp.concatenate([picked[:HEAD_ROWS], picked[HEAD_ROWS:]], axis=1)
        queries = joined[:HQ]
        new_key = joined[HQ : HQ + 1]
        new_value = joined[HQ + 1 : HQ + 2]
        inv_rms = inverse[pl.ds(model * SHARE + row, 1), :][:, :1]
        scores = lax.dot_general(
            queries.astype(jnp.bfloat16), key_buf[row], (((1,), (1,)), ((), ())),
            preferred_element_type=jnp.float32,
        ) * (inv_rms / math.sqrt(HD))
        own_score = jnp.sum(queries * new_key, axis=1, keepdims=True) * (
            inv_rms * inv_rms / math.sqrt(HD)
        )
        valid = positions < lengths_ref[row]
        scores = jnp.where(valid, scores, NEG_FILL)
        row_max = jnp.maximum(jnp.max(scores, axis=1, keepdims=True), own_score)
        weights = jnp.where(valid, jnp.exp(scores - row_max), 0.0)
        own_weight = jnp.exp(own_score - row_max)
        denominator = jnp.sum(weights, axis=1, keepdims=True) + own_weight
        weighted = jnp.dot(
            weights.astype(jnp.bfloat16), value_buf[row], preferred_element_type=jnp.float32
        )
        weighted = weighted + own_weight * inv_rms * new_value
        out_ref[row] = (weighted / denominator).astype(jnp.bfloat16)

    @pl.loop(0, chunks)
    def _(k):
        for d in range(BATCH - 1):
            pl.when(sends_right(d))(lambda d=d: to_right(d, k).wait_send())
            pl.when(sends_left(d))(lambda d=d: to_left(d, k).wait_send())

    for step in range(1, MODEL):
        square_copy(step).wait_send()
    for j in range(pieces):
        core_copy(j).wait_send()
        x_copy(j).wait_send()
        for step in range(1, BATCH):
            z_copy(j, step).wait_send()


def fused_device(tokens, norm_gain, w_qkv, key_cache, value_cache, lengths):
    features, width = w_qkv.shape
    chunks = features // CHUNK
    pieces = width // PIECE_COLS
    dma = pltpu.SemaphoreType.DMA
    vmem = pl.BlockSpec(memory_space=pltpu.VMEM)
    hbm = pl.BlockSpec(memory_space=pl.ANY)
    hops = BATCH - 1
    context = pl.pallas_call(
        fused_kernel,
        out_shape=jax.ShapeDtypeStruct((SHARE, HQ, HD), jnp.bfloat16),
        in_specs=[pl.BlockSpec(memory_space=pltpu.SMEM), vmem, vmem, hbm, hbm, hbm],
        out_specs=vmem,
        scratch_shapes=[
            pltpu.VMEM((chunks, CHUNK, width), jnp.bfloat16),
            pltpu.VMEM(key_cache.shape, jnp.bfloat16),
            pltpu.VMEM(value_cache.shape, jnp.bfloat16),
            pltpu.VMEM((chunks, BATCH, 2 * ROWS, HALF), jnp.bfloat16),
            pltpu.VMEM((2 * BATCH * ROWS, 2 * BATCH * ROWS), jnp.bfloat16),
            pltpu.VMEM((BATCH * PIECE_ROWS, LANES), jnp.bfloat16),
            pltpu.VMEM((SHARE, 2 * HEAD_ROWS, BATCH * pieces * PIECE_ROWS), jnp.bfloat16),
            pltpu.VMEM((BATCH * ROWS, width), jnp.float32),
            pltpu.VMEM((pieces, 2 * ROWS, PIECE_COLS), jnp.float32),
            pltpu.VMEM((pieces, ROWS, PIECE_COLS), jnp.float32),
            pltpu.VMEM((pieces, ROWS, PIECE_COLS), jnp.float32),
            pltpu.VMEM((pieces, BATCH, PIECE_ROWS, LANES), jnp.bfloat16),
            pltpu.VMEM((BATCH, pieces, PIECE_ROWS, LANES), jnp.bfloat16),
            pltpu.VMEM((MODEL, ROWS, LANES), jnp.float32),
            pltpu.VMEM((ROWS, LANES), jnp.float32),
            dma((chunks,)), dma((2,)),
            dma((hops, chunks)), dma((hops, chunks)), dma((hops, chunks)), dma((hops, chunks)),
            dma((pieces,)), dma((pieces,)), dma((pieces,)), dma((pieces,)),
            dma((BATCH, pieces)), dma((BATCH, pieces)),
            dma((MODEL,)), dma((MODEL,)),
        ],
        compiler_params=pltpu.CompilerParams(
            collective_id=0, has_side_effects=True, vmem_limit_bytes=54 * 1024 * 1024
        ),
        name="qkv_attention",
    )(lengths, tokens, norm_gain, w_qkv, key_cache, value_cache)
    return context.reshape(SHARE, HQ * HD)


def per_device(tokens, norm_gain, w_qkv, key_cache, value_cache, lengths):
    fits = (
        lax.axis_size("batch") == BATCH
        and lax.axis_size("mp") == MODEL
        and tokens.shape[0] == ROWS
        and w_qkv.shape[0] % CHUNK == 0
        and w_qkv.shape[1] % PIECE_COLS == 0
        and w_qkv.shape[1] * BATCH == (HQ + 2) * HD
    )
    run = fused_device if fits else plain_device
    return run(tokens, norm_gain, w_qkv, key_cache, value_cache, lengths)


def solution(mesh):
    return jax.shard_map(
        per_device,
        mesh=mesh,
        in_specs=(
            P(("groups", "batch"), "mp"),
            P("mp"),
            P("mp", "batch"),
            P(("groups", "batch", "mp"), None, None),
            P(("groups", "batch", "mp"), None, None),
            P(("groups", "batch", "mp")),
        ),
        out_specs=P(("groups", "batch", "mp"), None),
        check_vma=False,
    )
```

```python
import math

import jax
import jax.numpy as jnp
from jax import lax
from jax.experimental import pallas as pl
from jax.experimental.pallas import tpu as pltpu
from jax.sharding import PartitionSpec as P

D = 18432
HQ = 48
HD = 256


EPSILON = 1e-06
NEG_FILL = -1e30

BATCH = 4
MODEL = 4
ROWS = 24
SHARE = 6
HALF = 256
CHUNK = 2 * HALF
LANES = 128
PIECE = 5
PIECE_COLS = PIECE * LANES
PIECE_ROWS = 32
HEAD_ROWS = 64
AHEAD = 4
LAG = 3
TOGETHER = 3
MESH_ID = pl.DeviceIdType.MESH


def attend(raw_qkv, inv_rms, key_cache, value_cache, lengths):
    row_count = raw_qkv.shape[0]
    queries = raw_qkv[:, : HQ * HD].reshape(row_count, HQ, HD)
    new_key = raw_qkv[:, HQ * HD : HQ * HD + HD]
    new_value = raw_qkv[:, HQ * HD + HD :]
    scale = inv_rms[:, None, None] / math.sqrt(HD)
    scores = (
        jnp.einsum("rhd,rpd->rhp", queries, key_cache, preferred_element_type=jnp.float32) * scale
    )
    own_score = (
        jnp.einsum("rhd,rd->rh", queries, new_key, preferred_element_type=jnp.float32)
        * (inv_rms * inv_rms / math.sqrt(HD))[:, None]
    )
    positions = jnp.arange(key_cache.shape[1], dtype=jnp.int32)
    valid_mask = (positions[None, :] < lengths[:, None])[:, None, :]
    scores = jnp.where(valid_mask, scores, NEG_FILL)
    row_max = jnp.maximum(jnp.max(scores, axis=2), own_score)
    weights = jnp.where(valid_mask, jnp.exp(scores - row_max[:, :, None]), 0.0)
    own_weight = jnp.exp(own_score - row_max)
    denominator = jnp.sum(weights, axis=2) + own_weight
    weights_low = weights.astype(jnp.bfloat16)
    weighted = jnp.einsum(
        "rhp,rpd->rhd", weights_low, value_cache, preferred_element_type=jnp.float32
    )
    weighted = (
        weighted
        + own_weight[:, :, None]
        * inv_rms[:, None, None]
        * new_value.astype(jnp.float32)[:, None, :]
    )
    context = weighted / denominator[:, :, None]
    return context.astype(jnp.bfloat16).reshape(row_count, HQ * HD)


def plain_device(tokens, norm_gain, w_qkv, key_cache, value_cache, lengths):
    widened = tokens.astype(jnp.float32)
    normed = (widened * norm_gain).astype(jnp.bfloat16)
    square_part = jnp.sum(widened * widened, axis=1)
    partial_value = jnp.dot(
        lax.all_gather(normed, "batch", axis=0, tiled=True),
        w_qkv,
        preferred_element_type=jnp.float32,
    )
    batch_count = lax.axis_size("batch")
    model_count = lax.axis_size("mp")
    row_total = tokens.shape[0]
    row_share = row_total // model_count
    col_width = w_qkv.shape[1]
    blocks = partial_value.reshape(batch_count, model_count, row_share, col_width)
    summed, square_sum = (
        lax.psum_scatter(blocks, "mp", scatter_dimension=1, tiled=True),
        lax.psum_scatter(
            square_part.reshape(1, model_count, row_share), "mp", scatter_dimension=1, tiled=True
        ),
    )
    arrived = lax.all_to_all(
        summed.astype(jnp.bfloat16), "batch", split_axis=0, concat_axis=3, tiled=True
    )
    raw_qkv = arrived.reshape(row_share, batch_count * col_width)
    square_sum = square_sum.reshape(row_share)
    inv_rms = 1.0 / jnp.sqrt(square_sum / D + EPSILON)
    return attend(raw_qkv, inv_rms, key_cache, value_cache, lengths)


def one_hot(source, width):
    lanes = lax.broadcasted_iota(jnp.int32, (source.shape[0], width), 1)
    return jnp.where(lanes == source, 1.0, 0.0).astype(jnp.bfloat16)


def row_index(count):
    return lax.broadcasted_iota(jnp.int32, (count, 1), 0)


def gather_matrix():
    index = row_index(2 * BATCH * ROWS)
    half = lax.div(index, BATCH * ROWS)
    place = lax.rem(index, BATCH * ROWS)
    core = lax.div(place, 2 * ROWS)
    along_x = lax.rem(lax.div(place, ROWS), 2)
    batch = lax.div(lax.rem(place, ROWS), SHARE)
    row = lax.rem(place, SHARE)
    source = batch * (2 * ROWS) + half * ROWS + (along_x * 2 + core) * SHARE + row
    return one_hot(source, 2 * BATCH * ROWS)


def scatter_matrix():
    index = row_index(BATCH * PIECE_ROWS)
    batch = lax.div(index, PIECE_ROWS)
    within = lax.rem(index, PIECE_ROWS)
    block = lax.div(within, SHARE)
    row = lax.rem(within, SHARE)
    source = jnp.where(within < PIECE * SHARE, block * ROWS + batch * SHARE + row, -1)
    return one_hot(source, LANES)


def head_matrix(row, width):
    index = row_index(2 * HEAD_ROWS)
    half = lax.div(index, HEAD_ROWS)
    head = lax.rem(index, HEAD_ROWS)
    block = head * 2 + half
    piece = lax.div(block, PIECE)
    source = piece * PIECE_ROWS + (block - piece * PIECE) * SHARE + row
    return one_hot(source, width)


def fused_kernel(
    lengths_ref, tokens_ref, gain_ref, w_ref, key_ref, value_ref, out_ref,
    w_buf, key_buf, value_buf, gathered, order, spread, heads, acc,
    core_in, x_out, x_in, z_out, z_in, squares, inverse,
    w_sem, cache_sem,
    right_send, right_recv, left_send, left_recv,
    core_send, core_recv, x_send, x_recv, z_send, z_recv, sq_send, sq_recv,
):
    group = lax.axis_index("groups")
    batch = lax.axis_index("batch")
    model = lax.axis_index("mp")
    core = lax.rem(model, 2)
    along_x = lax.div(model, 2)
    sibling = model + 1 - 2 * core
    across = lax.rem(model + 2, MODEL)
    chunks = w_ref.shape[0] // CHUNK
    pieces = w_ref.shape[1] // PIECE_COLS

    barrier = pltpu.get_barrier_semaphore()
    for step in range(1, BATCH):
        pl.semaphore_signal(
            barrier, inc=1, device_id=(group, lax.rem(batch + step, BATCH), model),
            device_id_type=MESH_ID,
        )
    for step in range(1, MODEL):
        pl.semaphore_signal(
            barrier, inc=1, device_id=(group, batch, lax.rem(model + step, MODEL)),
            device_id_type=MESH_ID,
        )

    def w_copy(k):
        return pltpu.make_async_copy(
            w_ref.at[pl.ds(pl.multiple_of(k * CHUNK, CHUNK), CHUNK)], w_buf.at[k], w_sem.at[k]
        )

    @pl.loop(0, chunks)
    def _(k):
        w_copy(k).start()

    key_copy = pltpu.make_async_copy(key_ref, key_buf, cache_sem.at[0])
    value_copy = pltpu.make_async_copy(value_ref, value_buf, cache_sem.at[1])
    key_copy.start()
    value_copy.start()

    total = jnp.zeros((ROWS, LANES), jnp.float32)
    for k in range(chunks):
        parts = []
        for half in range(2):
            columns = pl.ds(k * CHUNK + half * HALF, HALF)
            widened = tokens_ref[:, columns].astype(jnp.float32)
            parts.append(widened * gain_ref[columns][None, :])
            squared = widened * widened
            total = total + squared[:, :LANES] + squared[:, LANES:]
        gathered[k, batch] = jnp.concatenate(parts, axis=0).astype(jnp.bfloat16)
    squares[model] = jnp.broadcast_to(jnp.sum(total, axis=1, keepdims=True), (ROWS, LANES))

    pl.semaphore_wait(barrier, BATCH + MODEL - 2)

    def to_right(d, k):
        block = gathered.at[k, lax.max(batch - d, 0)]
        return pltpu.make_async_remote_copy(
            src_ref=block, dst_ref=block,
            send_sem=right_send.at[d, k], recv_sem=right_recv.at[d, k],
            device_id=(group, lax.min(batch + 1, BATCH - 1), model), device_id_type=MESH_ID,
        )

    def to_left(d, k):
        block = gathered.at[k, lax.min(batch + d, BATCH - 1)]
        return pltpu.make_async_remote_copy(
            src_ref=block, dst_ref=block,
            send_sem=left_send.at[d, k], recv_sem=left_recv.at[d, k],
            device_id=(group, lax.max(batch - 1, 0), model), device_id_type=MESH_ID,
        )

    def sends_right(d):
        return jnp.logical_and(batch >= d, batch < BATCH - 1)

    def sends_left(d):
        return jnp.logical_and(batch + d < BATCH, batch > 0)

    def send(d, k):
        pl.when(sends_right(d))(lambda: to_right(d, k).start())
        pl.when(sends_left(d))(lambda: to_left(d, k).start())

    def receive(d, k):
        incoming = gathered.at[k, 0]

        @pl.when(batch >= d + 1)
        def _():
            pltpu.make_async_remote_copy(
                src_ref=incoming, dst_ref=gathered.at[k, lax.max(batch - d - 1, 0)],
                send_sem=right_send.at[d, k], recv_sem=right_recv.at[d, k],
                device_id=(group, lax.max(batch - 1, 0), model), device_id_type=MESH_ID,
            ).wait_recv()
            if d + 1 < BATCH - 1:
                pl.when(batch < BATCH - 1)(lambda: to_right(d + 1, k).start())

        @pl.when(batch + d + 1 < BATCH)
        def _():
            pltpu.make_async_remote_copy(
                src_ref=incoming, dst_ref=gathered.at[k, lax.min(batch + d + 1, BATCH - 1)],
                send_sem=left_send.at[d, k], recv_sem=left_recv.at[d, k],
                device_id=(group, lax.min(batch + 1, BATCH - 1), model), device_id_type=MESH_ID,
            ).wait_recv()
            if d + 1 < BATCH - 1:
                pl.when(batch > 0)(lambda: to_left(d + 1, k).start())

    for k in range(AHEAD):
        send(0, k)

    def square_copy(step):
        return pltpu.make_async_remote_copy(
            src_ref=squares.at[model], dst_ref=squares.at[model],
            send_sem=sq_send.at[step], recv_sem=sq_recv.at[step],
            device_id=(group, batch, lax.rem(model + step, MODEL)), device_id_type=MESH_ID,
        )

    for step in range(1, MODEL):
        square_copy(step).start()

    order[...] = gather_matrix()
    spread[...] = scatter_matrix()
    for row in range(SHARE):
        heads[row] = head_matrix(row, heads.shape[2])

    def left_side(k):
        arrived = gathered[k].reshape(2 * BATCH * ROWS, HALF)
        ordered = jnp.dot(order[...], arrived, preferred_element_type=jnp.float32)
        ordered = ordered.astype(jnp.bfloat16)
        return jnp.concatenate([ordered[: BATCH * ROWS], ordered[BATCH * ROWS :]], axis=1)

    acc[...] = jnp.zeros_like(acc)

    width = w_ref.shape[1]
    tile = 3 * HD

    @pl.loop(0, chunks - 1 + 2 * LAG)
    def _(it):
        pl.when(it + AHEAD < chunks)(lambda: send(0, it + AHEAD))
        pl.when(it < chunks)(lambda: receive(0, it))
        pl.when(jnp.logical_and(it >= LAG, it < chunks + LAG))(lambda: receive(1, it - LAG))

        @pl.when(it >= 2 * LAG)
        def _():
            k = it - 2 * LAG
            receive(2, k)
            w_copy(k).wait()
            left = left_side(k)
            start = 0
            while start < width:
                stop = width if width - start < 2 * tile - LANES else start + tile
                acc[:, start:stop] += jnp.dot(
                    left, w_buf[k, :, start:stop], preferred_element_type=jnp.float32
                )
                start = stop

    last = chunks - 1
    receive(2, last)
    w_copy(last).wait()
    left = left_side(last)

    def half_rows(which):
        return pl.ds(pl.multiple_of(which * (2 * ROWS), 8), 2 * ROWS)

    def core_copy(j):
        return pltpu.make_async_remote_copy(
            src_ref=acc.at[half_rows(1 - core), pl.ds(j * PIECE_COLS, PIECE_COLS)],
            dst_ref=core_in.at[j],
            send_sem=core_send.at[j], recv_sem=core_recv.at[j],
            device_id=(group, batch, sibling), device_id_type=MESH_ID,
        )

    def x_copy(j):
        return pltpu.make_async_remote_copy(
            src_ref=x_out.at[j], dst_ref=x_in.at[j],
            send_sem=x_send.at[j], recv_sem=x_recv.at[j],
            device_id=(group, batch, across), device_id_type=MESH_ID,
        )

    def z_copy(j, step):
        other = lax.rem(batch + step, BATCH)
        return pltpu.make_async_remote_copy(
            src_ref=z_out.at[j, other], dst_ref=z_in.at[batch, j],
            send_sem=z_send.at[step, j], recv_sem=z_recv.at[step, j],
            device_id=(group, other, model), device_id_type=MESH_ID,
        )

    def pair_sum(j, which):
        rows = pl.ds(pl.multiple_of(core * (2 * ROWS) + which * ROWS, 8), ROWS)
        own = acc[rows, pl.ds(j * PIECE_COLS, PIECE_COLS)]
        return own + core_in[j, pl.ds(pl.multiple_of(which * ROWS, 8), ROWS)]

    def pass_across(j):
        core_copy(j).wait_recv()
        x_out[j] = pair_sum(j, 1 - along_x)
        x_copy(j).start()

    for j in range(pieces):
        columns = slice(j * PIECE_COLS, (j + 1) * PIECE_COLS)
        acc[:, columns] += jnp.dot(
            left, w_buf[last, :, columns], preferred_element_type=jnp.float32
        )
        core_copy(j).start()
        if j:
            pass_across(j - 1)
    pass_across(pieces - 1)

    for j in range(pieces):
        x_copy(j).wait_recv()
        final = pair_sum(j, along_x) + x_in[j]
        blocks = [final[:, h * LANES : (h + 1) * LANES] for h in range(PIECE)]
        blocks.append(jnp.zeros((LANES - PIECE * ROWS, LANES), jnp.float32))
        stacked = jnp.concatenate(blocks, axis=0).astype(jnp.bfloat16)
        placed = jnp.dot(spread[...], stacked, preferred_element_type=jnp.float32)
        z_out[j] = placed.astype(jnp.bfloat16).reshape(BATCH, PIECE_ROWS, LANES)
        for step in range(1, BATCH):
            z_copy(j, step).start()
        z_in[batch, j] = z_out[j, batch]

    for step in range(1, MODEL):
        square_copy(step).wait_recv()
    square_sum = squares[0] + squares[1] + squares[2] + squares[3]
    inverse[...] = 1.0 / jnp.sqrt(square_sum / D + EPSILON)
    key_copy.wait()
    value_copy.wait()
    for j in range(pieces):
        for step in range(1, BATCH):
            z_copy(j, step).wait_recv()

    columns = z_in[...].reshape(BATCH * pieces * PIECE_ROWS, LANES)
    positions = lax.broadcasted_iota(jnp.int32, (HQ, key_ref.shape[1]), 1)

    def score(row):
        picked = jnp.dot(heads[row], columns, preferred_element_type=jnp.float32)
        joined = jnp.concatenate([picked[:HEAD_ROWS], picked[HEAD_ROWS:]], axis=1)
        queries = joined[:HQ]
        new_key = joined[HQ : HQ + 1]
        new_value = joined[HQ + 1 : HQ + 2]
        inv_rms = inverse[pl.ds(model * SHARE + row, 1), :][:, :1]
        scores = lax.dot_general(
            queries.astype(jnp.bfloat16), key_buf[row], (((1,), (1,)), ((), ())),
            preferred_element_type=jnp.float32,
        ) * (inv_rms / math.sqrt(HD))
        own_score = jnp.sum(queries * new_key, axis=1, keepdims=True) * (
            inv_rms * inv_rms / math.sqrt(HD)
        )
        return scores, own_score, inv_rms * new_value

    def soften(row, scores, own_score):
        valid = positions < lengths_ref[row]
        scores = jnp.where(valid, scores, NEG_FILL)
        row_max = jnp.maximum(jnp.max(scores, axis=1, keepdims=True), own_score)
        weights = jnp.where(valid, jnp.exp(scores - row_max), 0.0)
        own_weight = jnp.exp(own_score - row_max)
        denominator = jnp.sum(weights, axis=1, keepdims=True) + own_weight
        return weights.astype(jnp.bfloat16), own_weight, denominator

    def combine(row, weights_low, own_weight, denominator, own_value):
        weighted = jnp.dot(weights_low, value_buf[row], preferred_element_type=jnp.float32)
        return ((weighted + own_weight * own_value) / denominator).astype(jnp.bfloat16)

    for first in range(0, SHARE, TOGETHER):
        rows = range(first, first + TOGETHER)
        scored = [score(row) for row in rows]
        softened = [soften(row, *scored[row - first][:2]) for row in rows]
        contexts = [
            combine(row, *softened[row - first], scored[row - first][2]) for row in rows
        ]
        for row in rows:
            out_ref[row] = contexts[row - first]

    @pl.loop(0, chunks)
    def _(k):
        for d in range(BATCH - 1):
            pl.when(sends_right(d))(lambda d=d: to_right(d, k).wait_send())
            pl.when(sends_left(d))(lambda d=d: to_left(d, k).wait_send())

    for step in range(1, MODEL):
        square_copy(step).wait_send()
    for j in range(pieces):
        core_copy(j).wait_send()
        x_copy(j).wait_send()
        for step in range(1, BATCH):
            z_copy(j, step).wait_send()


def fused_device(tokens, norm_gain, w_qkv, key_cache, value_cache, lengths):
    features, width = w_qkv.shape
    chunks = features // CHUNK
    pieces = width // PIECE_COLS
    dma = pltpu.SemaphoreType.DMA
    vmem = pl.BlockSpec(memory_space=pltpu.VMEM)
    hbm = pl.BlockSpec(memory_space=pl.ANY)
    hops = BATCH - 1
    context = pl.pallas_call(
        fused_kernel,
        out_shape=jax.ShapeDtypeStruct((SHARE, HQ, HD), jnp.bfloat16),
        in_specs=[pl.BlockSpec(memory_space=pltpu.SMEM), vmem, vmem, hbm, hbm, hbm],
        out_specs=vmem,
        scratch_shapes=[
            pltpu.VMEM((chunks, CHUNK, width), jnp.bfloat16),
            pltpu.VMEM(key_cache.shape, jnp.bfloat16),
            pltpu.VMEM(value_cache.shape, jnp.bfloat16),
            pltpu.VMEM((chunks, BATCH, 2 * ROWS, HALF), jnp.bfloat16),
            pltpu.VMEM((2 * BATCH * ROWS, 2 * BATCH * ROWS), jnp.bfloat16),
            pltpu.VMEM((BATCH * PIECE_ROWS, LANES), jnp.bfloat16),
            pltpu.VMEM((SHARE, 2 * HEAD_ROWS, BATCH * pieces * PIECE_ROWS), jnp.bfloat16),
            pltpu.VMEM((BATCH * ROWS, width), jnp.float32),
            pltpu.VMEM((pieces, 2 * ROWS, PIECE_COLS), jnp.float32),
            pltpu.VMEM((pieces, ROWS, PIECE_COLS), jnp.float32),
            pltpu.VMEM((pieces, ROWS, PIECE_COLS), jnp.float32),
            pltpu.VMEM((pieces, BATCH, PIECE_ROWS, LANES), jnp.bfloat16),
            pltpu.VMEM((BATCH, pieces, PIECE_ROWS, LANES), jnp.bfloat16),
            pltpu.VMEM((MODEL, ROWS, LANES), jnp.float32),
            pltpu.VMEM((ROWS, LANES), jnp.float32),
            dma((chunks,)), dma((2,)),
            dma((hops, chunks)), dma((hops, chunks)), dma((hops, chunks)), dma((hops, chunks)),
            dma((pieces,)), dma((pieces,)), dma((pieces,)), dma((pieces,)),
            dma((BATCH, pieces)), dma((BATCH, pieces)),
            dma((MODEL,)), dma((MODEL,)),
        ],
        compiler_params=pltpu.CompilerParams(
            collective_id=0, has_side_effects=True, vmem_limit_bytes=54 * 1024 * 1024
        ),
        name="qkv_attention",
    )(lengths, tokens, norm_gain, w_qkv, key_cache, value_cache)
    return context.reshape(SHARE, HQ * HD)


def per_device(tokens, norm_gain, w_qkv, key_cache, value_cache, lengths):
    fits = (
        lax.axis_size("batch") == BATCH
        and lax.axis_size("mp") == MODEL
        and tokens.shape[0] == ROWS
        and w_qkv.shape[0] % CHUNK == 0
        and w_qkv.shape[1] % PIECE_COLS == 0
        and w_qkv.shape[1] * BATCH == (HQ + 2) * HD
    )
    run = fused_device if fits else plain_device
    return run(tokens, norm_gain, w_qkv, key_cache, value_cache, lengths)


def solution(mesh):
    return jax.shard_map(
        per_device,
        mesh=mesh,
        in_specs=(
            P(("groups", "batch"), "mp"),
            P("mp"),
            P("mp", "batch"),
            P(("groups", "batch", "mp"), None, None),
            P(("groups", "batch", "mp"), None, None),
            P(("groups", "batch", "mp")),
        ),
        out_specs=P(("groups", "batch", "mp"), None),
        check_vma=False,
    )
```

```python
import math

import jax
import jax.numpy as jnp
from jax import lax
from jax.experimental import pallas as pl
from jax.experimental.pallas import tpu as pltpu
from jax.sharding import PartitionSpec as P

D = 18432
HQ = 48
HD = 256


EPSILON = 1e-06
NEG_FILL = -1e30

BATCH = 4
MODEL = 4
ROWS = 24
SHARE = 6
HALF = 384
CHUNK = 2 * HALF
LANES = 128
PIECE = 5
PIECE_COLS = PIECE * LANES
PIECE_ROWS = 32
HEAD_ROWS = 64
AHEAD = 3
LAG = 2
TOGETHER = 3
MESH_ID = pl.DeviceIdType.MESH


def attend(raw_qkv, inv_rms, key_cache, value_cache, lengths):
    row_count = raw_qkv.shape[0]
    queries = raw_qkv[:, : HQ * HD].reshape(row_count, HQ, HD)
    new_key = raw_qkv[:, HQ * HD : HQ * HD + HD]
    new_value = raw_qkv[:, HQ * HD + HD :]
    scale = inv_rms[:, None, None] / math.sqrt(HD)
    scores = (
        jnp.einsum("rhd,rpd->rhp", queries, key_cache, preferred_element_type=jnp.float32) * scale
    )
    own_score = (
        jnp.einsum("rhd,rd->rh", queries, new_key, preferred_element_type=jnp.float32)
        * (inv_rms * inv_rms / math.sqrt(HD))[:, None]
    )
    positions = jnp.arange(key_cache.shape[1], dtype=jnp.int32)
    valid_mask = (positions[None, :] < lengths[:, None])[:, None, :]
    scores = jnp.where(valid_mask, scores, NEG_FILL)
    row_max = jnp.maximum(jnp.max(scores, axis=2), own_score)
    weights = jnp.where(valid_mask, jnp.exp(scores - row_max[:, :, None]), 0.0)
    own_weight = jnp.exp(own_score - row_max)
    denominator = jnp.sum(weights, axis=2) + own_weight
    weights_low = weights.astype(jnp.bfloat16)
    weighted = jnp.einsum(
        "rhp,rpd->rhd", weights_low, value_cache, preferred_element_type=jnp.float32
    )
    weighted = (
        weighted
        + own_weight[:, :, None]
        * inv_rms[:, None, None]
        * new_value.astype(jnp.float32)[:, None, :]
    )
    context = weighted / denominator[:, :, None]
    return context.astype(jnp.bfloat16).reshape(row_count, HQ * HD)


def plain_device(tokens, norm_gain, w_qkv, key_cache, value_cache, lengths):
    widened = tokens.astype(jnp.float32)
    normed = (widened * norm_gain).astype(jnp.bfloat16)
    square_part = jnp.sum(widened * widened, axis=1)
    partial_value = jnp.dot(
        lax.all_gather(normed, "batch", axis=0, tiled=True),
        w_qkv,
        preferred_element_type=jnp.float32,
    )
    batch_count = lax.axis_size("batch")
    model_count = lax.axis_size("mp")
    row_total = tokens.shape[0]
    row_share = row_total // model_count
    col_width = w_qkv.shape[1]
    blocks = partial_value.reshape(batch_count, model_count, row_share, col_width)
    summed, square_sum = (
        lax.psum_scatter(blocks, "mp", scatter_dimension=1, tiled=True),
        lax.psum_scatter(
            square_part.reshape(1, model_count, row_share), "mp", scatter_dimension=1, tiled=True
        ),
    )
    arrived = lax.all_to_all(
        summed.astype(jnp.bfloat16), "batch", split_axis=0, concat_axis=3, tiled=True
    )
    raw_qkv = arrived.reshape(row_share, batch_count * col_width)
    square_sum = square_sum.reshape(row_share)
    inv_rms = 1.0 / jnp.sqrt(square_sum / D + EPSILON)
    return attend(raw_qkv, inv_rms, key_cache, value_cache, lengths)


def one_hot(source, width):
    lanes = lax.broadcasted_iota(jnp.int32, (source.shape[0], width), 1)
    return jnp.where(lanes == source, 1.0, 0.0).astype(jnp.bfloat16)


def row_index(count):
    return lax.broadcasted_iota(jnp.int32, (count, 1), 0)


def gather_matrix():
    index = row_index(2 * BATCH * ROWS)
    half = lax.div(index, BATCH * ROWS)
    place = lax.rem(index, BATCH * ROWS)
    core = lax.div(place, 2 * ROWS)
    along_x = lax.rem(lax.div(place, ROWS), 2)
    batch = lax.div(lax.rem(place, ROWS), SHARE)
    row = lax.rem(place, SHARE)
    source = batch * (2 * ROWS) + half * ROWS + (along_x * 2 + core) * SHARE + row
    return one_hot(source, 2 * BATCH * ROWS)


def scatter_matrix():
    index = row_index(BATCH * PIECE_ROWS)
    batch = lax.div(index, PIECE_ROWS)
    within = lax.rem(index, PIECE_ROWS)
    block = lax.div(within, SHARE)
    row = lax.rem(within, SHARE)
    source = jnp.where(within < PIECE * SHARE, block * ROWS + batch * SHARE + row, -1)
    return one_hot(source, LANES)


def head_matrix(row, width):
    index = row_index(2 * HEAD_ROWS)
    half = lax.div(index, HEAD_ROWS)
    head = lax.rem(index, HEAD_ROWS)
    block = head * 2 + half
    piece = lax.div(block, PIECE)
    source = piece * PIECE_ROWS + (block - piece * PIECE) * SHARE + row
    return one_hot(source, width)


def fused_kernel(
    lengths_ref, tokens_ref, gain_ref, w_ref, key_ref, value_ref, out_ref,
    w_buf, key_buf, value_buf, gathered, order, spread, heads, acc,
    core_in, x_out, x_in, z_out, z_in, squares, inverse,
    w_sem, cache_sem,
    right_send, right_recv, left_send, left_recv,
    core_send, core_recv, x_send, x_recv, z_send, z_recv, sq_send, sq_recv,
):
    group = lax.axis_index("groups")
    batch = lax.axis_index("batch")
    model = lax.axis_index("mp")
    core = lax.rem(model, 2)
    along_x = lax.div(model, 2)
    sibling = model + 1 - 2 * core
    across = lax.rem(model + 2, MODEL)
    chunks = w_ref.shape[0] // CHUNK
    pieces = w_ref.shape[1] // PIECE_COLS

    barrier = pltpu.get_barrier_semaphore()
    for step in range(1, BATCH):
        pl.semaphore_signal(
            barrier, inc=1, device_id=(group, lax.rem(batch + step, BATCH), model),
            device_id_type=MESH_ID,
        )
    for step in range(1, MODEL):
        pl.semaphore_signal(
            barrier, inc=1, device_id=(group, batch, lax.rem(model + step, MODEL)),
            device_id_type=MESH_ID,
        )

    def w_copy(k):
        return pltpu.make_async_copy(
            w_ref.at[pl.ds(pl.multiple_of(k * CHUNK, CHUNK), CHUNK)], w_buf.at[k], w_sem.at[k]
        )

    @pl.loop(0, chunks)
    def _(k):
        w_copy(k).start()

    key_copy = pltpu.make_async_copy(key_ref, key_buf, cache_sem.at[0])
    value_copy = pltpu.make_async_copy(value_ref, value_buf, cache_sem.at[1])
    key_copy.start()
    value_copy.start()

    total = jnp.zeros((ROWS, LANES), jnp.float32)
    for k in range(chunks):
        parts = []
        for half in range(2):
            columns = pl.ds(k * CHUNK + half * HALF, HALF)
            widened = tokens_ref[:, columns].astype(jnp.float32)
            parts.append(widened * gain_ref[columns][None, :])
            squared = widened * widened
            for start in range(0, HALF, LANES):
                total = total + squared[:, start : start + LANES]
        gathered[k, batch] = jnp.concatenate(parts, axis=0).astype(jnp.bfloat16)
    squares[model] = jnp.broadcast_to(jnp.sum(total, axis=1, keepdims=True), (ROWS, LANES))

    pl.semaphore_wait(barrier, BATCH + MODEL - 2)

    def to_right(d, k):
        block = gathered.at[k, lax.max(batch - d, 0)]
        return pltpu.make_async_remote_copy(
            src_ref=block, dst_ref=block,
            send_sem=right_send.at[d, k], recv_sem=right_recv.at[d, k],
            device_id=(group, lax.min(batch + 1, BATCH - 1), model), device_id_type=MESH_ID,
        )

    def to_left(d, k):
        block = gathered.at[k, lax.min(batch + d, BATCH - 1)]
        return pltpu.make_async_remote_copy(
            src_ref=block, dst_ref=block,
            send_sem=left_send.at[d, k], recv_sem=left_recv.at[d, k],
            device_id=(group, lax.max(batch - 1, 0), model), device_id_type=MESH_ID,
        )

    def sends_right(d):
        return jnp.logical_and(batch >= d, batch < BATCH - 1)

    def sends_left(d):
        return jnp.logical_and(batch + d < BATCH, batch > 0)

    def send(d, k):
        pl.when(sends_right(d))(lambda: to_right(d, k).start())
        pl.when(sends_left(d))(lambda: to_left(d, k).start())

    def receive(d, k):
        incoming = gathered.at[k, 0]

        @pl.when(batch >= d + 1)
        def _():
            pltpu.make_async_remote_copy(
                src_ref=incoming, dst_ref=gathered.at[k, lax.max(batch - d - 1, 0)],
                send_sem=right_send.at[d, k], recv_sem=right_recv.at[d, k],
                device_id=(group, lax.max(batch - 1, 0), model), device_id_type=MESH_ID,
            ).wait_recv()
            if d + 1 < BATCH - 1:
                pl.when(batch < BATCH - 1)(lambda: to_right(d + 1, k).start())

        @pl.when(batch + d + 1 < BATCH)
        def _():
            pltpu.make_async_remote_copy(
                src_ref=incoming, dst_ref=gathered.at[k, lax.min(batch + d + 1, BATCH - 1)],
                send_sem=left_send.at[d, k], recv_sem=left_recv.at[d, k],
                device_id=(group, lax.min(batch + 1, BATCH - 1), model), device_id_type=MESH_ID,
            ).wait_recv()
            if d + 1 < BATCH - 1:
                pl.when(batch > 0)(lambda: to_left(d + 1, k).start())

    for k in range(AHEAD):
        send(0, k)

    def square_copy(step):
        return pltpu.make_async_remote_copy(
            src_ref=squares.at[model], dst_ref=squares.at[model],
            send_sem=sq_send.at[step], recv_sem=sq_recv.at[step],
            device_id=(group, batch, lax.rem(model + step, MODEL)), device_id_type=MESH_ID,
        )

    for step in range(1, MODEL):
        square_copy(step).start()

    order[...] = gather_matrix()
    spread[...] = scatter_matrix()
    for row in range(SHARE):
        heads[row] = head_matrix(row, heads.shape[2])

    def left_side(k):
        arrived = gathered[k].reshape(2 * BATCH * ROWS, HALF)
        ordered = jnp.dot(order[...], arrived, preferred_element_type=jnp.float32)
        ordered = ordered.astype(jnp.bfloat16)
        return jnp.concatenate([ordered[: BATCH * ROWS], ordered[BATCH * ROWS :]], axis=1)

    acc[...] = jnp.zeros_like(acc)

    width = w_ref.shape[1]
    tile = 3 * HD

    @pl.loop(0, chunks - 1 + 2 * LAG)
    def _(it):
        pl.when(it + AHEAD < chunks)(lambda: send(0, it + AHEAD))
        pl.when(it < chunks)(lambda: receive(0, it))
        pl.when(jnp.logical_and(it >= LAG, it < chunks + LAG))(lambda: receive(1, it - LAG))

        @pl.when(it >= 2 * LAG)
        def _():
            k = it - 2 * LAG
            receive(2, k)
            w_copy(k).wait()
            left = left_side(k)
            start = 0
            while start < width:
                stop = width if width - start < 2 * tile - LANES else start + tile
                acc[:, start:stop] += jnp.dot(
                    left, w_buf[k, :, start:stop], preferred_element_type=jnp.float32
                )
                start = stop

    last = chunks - 1
    receive(2, last)
    w_copy(last).wait()
    left = left_side(last)

    def half_rows(which):
        return pl.ds(pl.multiple_of(which * (2 * ROWS), 8), 2 * ROWS)

    def core_copy(j):
        return pltpu.make_async_remote_copy(
            src_ref=acc.at[half_rows(1 - core), pl.ds(j * PIECE_COLS, PIECE_COLS)],
            dst_ref=core_in.at[j],
            send_sem=core_send.at[j], recv_sem=core_recv.at[j],
            device_id=(group, batch, sibling), device_id_type=MESH_ID,
        )

    def x_copy(j):
        return pltpu.make_async_remote_copy(
            src_ref=x_out.at[j], dst_ref=x_in.at[j],
            send_sem=x_send.at[j], recv_sem=x_recv.at[j],
            device_id=(group, batch, across), device_id_type=MESH_ID,
        )

    def z_copy(j, step):
        other = lax.rem(batch + step, BATCH)
        return pltpu.make_async_remote_copy(
            src_ref=z_out.at[j, other], dst_ref=z_in.at[batch, j],
            send_sem=z_send.at[step, j], recv_sem=z_recv.at[step, j],
            device_id=(group, other, model), device_id_type=MESH_ID,
        )

    def pair_sum(j, which):
        rows = pl.ds(pl.multiple_of(core * (2 * ROWS) + which * ROWS, 8), ROWS)
        own = acc[rows, pl.ds(j * PIECE_COLS, PIECE_COLS)]
        return own + core_in[j, pl.ds(pl.multiple_of(which * ROWS, 8), ROWS)]

    def pass_across(j):
        core_copy(j).wait_recv()
        x_out[j] = pair_sum(j, 1 - along_x)
        x_copy(j).start()

    for j in range(pieces):
        columns = slice(j * PIECE_COLS, (j + 1) * PIECE_COLS)
        acc[:, columns] += jnp.dot(
            left, w_buf[last, :, columns], preferred_element_type=jnp.float32
        )
        core_copy(j).start()
        if j:
            pass_across(j - 1)
    pass_across(pieces - 1)

    for j in range(pieces):
        x_copy(j).wait_recv()
        final = pair_sum(j, along_x) + x_in[j]
        blocks = [final[:, h * LANES : (h + 1) * LANES] for h in range(PIECE)]
        blocks.append(jnp.zeros((LANES - PIECE * ROWS, LANES), jnp.float32))
        stacked = jnp.concatenate(blocks, axis=0).astype(jnp.bfloat16)
        placed = jnp.dot(spread[...], stacked, preferred_element_type=jnp.float32)
        z_out[j] = placed.astype(jnp.bfloat16).reshape(BATCH, PIECE_ROWS, LANES)
        for step in range(1, BATCH):
            z_copy(j, step).start()
        z_in[batch, j] = z_out[j, batch]

    for step in range(1, MODEL):
        square_copy(step).wait_recv()
    square_sum = squares[0] + squares[1] + squares[2] + squares[3]
    inverse[...] = 1.0 / jnp.sqrt(square_sum / D + EPSILON)
    key_copy.wait()
    value_copy.wait()
    for j in range(pieces):
        for step in range(1, BATCH):
            z_copy(j, step).wait_recv()

    columns = z_in[...].reshape(BATCH * pieces * PIECE_ROWS, LANES)
    positions = lax.broadcasted_iota(jnp.int32, (HQ, key_ref.shape[1]), 1)

    def score(row):
        picked = jnp.dot(heads[row], columns, preferred_element_type=jnp.float32)
        joined = jnp.concatenate([picked[:HEAD_ROWS], picked[HEAD_ROWS:]], axis=1)
        queries = joined[:HQ]
        new_key = joined[HQ : HQ + 1]
        new_value = joined[HQ + 1 : HQ + 2]
        inv_rms = inverse[pl.ds(model * SHARE + row, 1), :][:, :1]
        scores = lax.dot_general(
            queries.astype(jnp.bfloat16), key_buf[row], (((1,), (1,)), ((), ())),
            preferred_element_type=jnp.float32,
        ) * (inv_rms / math.sqrt(HD))
        own_score = jnp.sum(queries * new_key, axis=1, keepdims=True) * (
            inv_rms * inv_rms / math.sqrt(HD)
        )
        return scores, own_score, inv_rms * new_value

    def soften(row, scores, own_score):
        valid = positions < lengths_ref[row]
        scores = jnp.where(valid, scores, NEG_FILL)
        row_max = jnp.maximum(jnp.max(scores, axis=1, keepdims=True), own_score)
        weights = jnp.where(valid, jnp.exp(scores - row_max), 0.0)
        own_weight = jnp.exp(own_score - row_max)
        denominator = jnp.sum(weights, axis=1, keepdims=True) + own_weight
        return weights.astype(jnp.bfloat16), own_weight, denominator

    def combine(row, weights_low, own_weight, denominator, own_value):
        weighted = jnp.dot(weights_low, value_buf[row], preferred_element_type=jnp.float32)
        return ((weighted + own_weight * own_value) / denominator).astype(jnp.bfloat16)

    for first in range(0, SHARE, TOGETHER):
        rows = range(first, first + TOGETHER)
        scored = [score(row) for row in rows]
        softened = [soften(row, *scored[row - first][:2]) for row in rows]
        contexts = [
            combine(row, *softened[row - first], scored[row - first][2]) for row in rows
        ]
        for row in rows:
            out_ref[row] = contexts[row - first]

    @pl.loop(0, chunks)
    def _(k):
        for d in range(BATCH - 1):
            pl.when(sends_right(d))(lambda d=d: to_right(d, k).wait_send())
            pl.when(sends_left(d))(lambda d=d: to_left(d, k).wait_send())

    for step in range(1, MODEL):
        square_copy(step).wait_send()
    for j in range(pieces):
        core_copy(j).wait_send()
        x_copy(j).wait_send()
        for step in range(1, BATCH):
            z_copy(j, step).wait_send()


def fused_device(tokens, norm_gain, w_qkv, key_cache, value_cache, lengths):
    features, width = w_qkv.shape
    chunks = features // CHUNK
    pieces = width // PIECE_COLS
    dma = pltpu.SemaphoreType.DMA
    vmem = pl.BlockSpec(memory_space=pltpu.VMEM)
    hbm = pl.BlockSpec(memory_space=pl.ANY)
    hops = BATCH - 1
    context = pl.pallas_call(
        fused_kernel,
        out_shape=jax.ShapeDtypeStruct((SHARE, HQ, HD), jnp.bfloat16),
        in_specs=[pl.BlockSpec(memory_space=pltpu.SMEM), vmem, vmem, hbm, hbm, hbm],
        out_specs=vmem,
        scratch_shapes=[
            pltpu.VMEM((chunks, CHUNK, width), jnp.bfloat16),
            pltpu.VMEM(key_cache.shape, jnp.bfloat16),
            pltpu.VMEM(value_cache.shape, jnp.bfloat16),
            pltpu.VMEM((chunks, BATCH, 2 * ROWS, HALF), jnp.bfloat16),
            pltpu.VMEM((2 * BATCH * ROWS, 2 * BATCH * ROWS), jnp.bfloat16),
            pltpu.VMEM((BATCH * PIECE_ROWS, LANES), jnp.bfloat16),
            pltpu.VMEM((SHARE, 2 * HEAD_ROWS, BATCH * pieces * PIECE_ROWS), jnp.bfloat16),
            pltpu.VMEM((BATCH * ROWS, width), jnp.float32),
            pltpu.VMEM((pieces, 2 * ROWS, PIECE_COLS), jnp.float32),
            pltpu.VMEM((pieces, ROWS, PIECE_COLS), jnp.float32),
            pltpu.VMEM((pieces, ROWS, PIECE_COLS), jnp.float32),
            pltpu.VMEM((pieces, BATCH, PIECE_ROWS, LANES), jnp.bfloat16),
            pltpu.VMEM((BATCH, pieces, PIECE_ROWS, LANES), jnp.bfloat16),
            pltpu.VMEM((MODEL, ROWS, LANES), jnp.float32),
            pltpu.VMEM((ROWS, LANES), jnp.float32),
            dma((chunks,)), dma((2,)),
            dma((hops, chunks)), dma((hops, chunks)), dma((hops, chunks)), dma((hops, chunks)),
            dma((pieces,)), dma((pieces,)), dma((pieces,)), dma((pieces,)),
            dma((BATCH, pieces)), dma((BATCH, pieces)),
            dma((MODEL,)), dma((MODEL,)),
        ],
        compiler_params=pltpu.CompilerParams(
            collective_id=0, has_side_effects=True, vmem_limit_bytes=54 * 1024 * 1024
        ),
        name="qkv_attention",
    )(lengths, tokens, norm_gain, w_qkv, key_cache, value_cache)
    return context.reshape(SHARE, HQ * HD)


def per_device(tokens, norm_gain, w_qkv, key_cache, value_cache, lengths):
    fits = (
        lax.axis_size("batch") == BATCH
        and lax.axis_size("mp") == MODEL
        and tokens.shape[0] == ROWS
        and w_qkv.shape[0] % CHUNK == 0
        and w_qkv.shape[1] % PIECE_COLS == 0
        and w_qkv.shape[1] * BATCH == (HQ + 2) * HD
    )
    run = fused_device if fits else plain_device
    return run(tokens, norm_gain, w_qkv, key_cache, value_cache, lengths)


def solution(mesh):
    return jax.shard_map(
        per_device,
        mesh=mesh,
        in_specs=(
            P(("groups", "batch"), "mp"),
            P("mp"),
            P("mp", "batch"),
            P(("groups", "batch", "mp"), None, None),
            P(("groups", "batch", "mp"), None, None),
            P(("groups", "batch", "mp")),
        ),
        out_specs=P(("groups", "batch", "mp"), None),
        check_vma=False,
    )
```
